512 devices in a mesh: seg: 64 (over z_lo, x, core), vec: 8 (over y, z_hi).
Axes of the slice: x: 4, y: 4, z: 16 (z_hi: 2, z_lo: 8; z = z_hi * 8 + z_lo), core: 2. Of those that a mesh axis runs over, the one named last changes fastest.
Arguments:
- line_vectors: float32 [256, 393216], P('vec', 'seg')
- mode_vectors: float32 [256, 16384], P('vec', 'seg'), may hold values from -6 to 6
- line_diagonal: float32 [393216], P('seg'), may hold values from 2 to 4
- line_links: float32 [393216], P('seg'), may hold values from 0.2 to 0.9
- stiffness: float32 [16384], P('seg'), may hold values from 0.5 to 6
- coupling_tiles: bfloat16 [2816, 128, 256], P('seg'), may hold values from -0.1875 to 0.1875
- attachments: int32 [2816, 1], P('seg'), may hold values from 0 to 63; in each aligned block of 44 rows (0 to 43, 44 to 87, ...) at most 2 rows name the same one
- block_counts: int32 [64, 2], P('seg'), may hold values from 1 to 24, 44 in all within a row
Outputs:
- filtered_line: float32 [256, 393216], P('vec', 'seg')
- filtered_modes: float32 [256, 16384], P('vec', 'seg')
- gram_matrix: float32 [256, 256], P('vec')
The draws below stay inside these ranges and needn't reach their ends.
Inputs may be any that keep to these rules, and one draw needn't show every extreme that they name: `attachments`: among the 44 rows of one device no mode block is named more than 2 times; some mode blocks are named by none of them. `block_counts`: each row sums to 44; attachments of a device are listed by segment block in order.
All inputs are finite; a program needn't handle non-finite values.
Results may differ from the reference program's by a relative error of at most 0.0005.
The reference program's roundings to bfloat16 on the way (of `outgoing`) count: a program that leaves them out, or rounds other values in their place, can miss the bound.
Values may be sent and summed in bfloat16 or wider, within the bound.
A program may use at most 64 MiB of HBM per device.

```python
import math
import jax
import jax.numpy as jnp
import numpy as np
from jax import lax

PANEL = 128
PANELS = 24
SEG_DEV = 2
A_MAX = 24
MB = 256
VECS = 256
ROWS_DEV = 6144
STATES = 393216
MODES = 16384
ATT_DEV = 44
ATTACH = 2816
CAP = 2
N_SEG = 64


def draw_line_vectors(key, part):
    key = jax.random.fold_in(key, 11)
    key_noise, key_common, key_weight = jax.random.split(key, 3)
    noise = jax.random.normal(key_noise, (VECS, STATES), jnp.float32)
    weights = jax.random.uniform(key_weight, (VECS, 1), jnp.float32, 0.3, 1.0)
    common = jax.random.normal(key_common, (1, STATES), jnp.float32)
    return noise + weights * common


def block_levels(stream_key, extent, cuts, low, top_value):
    loudness, own = 1.0, jax.random.fold_in(stream_key, 6)
    for axis_at, blocks in cuts:
        heights = jnp.exp(jax.random.uniform(jax.random.fold_in(own, axis_at), (blocks,), jnp.float32, low / len(cuts), top_value / len(cuts)))
        loudness = loudness * jnp.repeat(heights, extent[axis_at] // blocks).reshape([-1 if axis == axis_at else 1 for axis in range(len(extent))])
    return loudness


def profile(amount, total, bound, skew):
    portions = [(1 << 20) // math.isqrt(grade ** skew) + 1 for grade in range(2, amount + 1)]
    spare, given = total - bound - (amount - 1), [1] * (amount - 1)
    while spare > 0:
        movable = [i for i in range(amount - 1) if given[i] < bound]
        whole, remaining = sum([portions[i] for i in movable]), spare
        for i in movable:
            more = min(bound - given[i], max(1, remaining * portions[i] // whole), spare)
            given[i] = given[i] + more
            spare = spare - more
    return np.array([bound] + given)


def ragged(own_key, number_of, total, limit, lean):
    if number_of == 2:
        one = jax.random.randint(own_key, (), max(1, total - limit), min(limit, total - 1) + 1)
        return jnp.stack([one, total - one])
    tallies = jnp.asarray(profile(number_of, total, limit, lean), jnp.int32)
    couples = (number_of - 1) // 2
    source_of, sink = tallies[1:1 + 2 * couples:2], tallies[2:2 + 2 * couples:2]
    margin = jnp.minimum(source_of - 1, limit - sink)
    moved = jax.random.randint(jax.random.fold_in(own_key, 1), (couples,), 0, 1 << 20) % (margin + 1)
    tallies = tallies.at[1:1 + 2 * couples:2].set(source_of - moved).at[2:2 + 2 * couples:2].set(sink + moved)
    return tallies[jax.random.permutation(jax.random.fold_in(own_key, 2), number_of)]


def deal_out(own_key, own, number, rows, number_of, top, reach, lean):
    order = jax.random.permutation(own_key, number_of)
    packed, usual = shares(number_of, rows * top, reach, lean, True), shares(number_of, rows * top, reach, lean, False)
    places = jnp.arange(number_of)

    def named(sizes, offset_by):
        used = int((sizes > 0).sum())
        fixed = max(1, used // 4)
        moved = fixed + (places - fixed + offset_by * (used - fixed)) % max(1, number_of - fixed)
        return jnp.zeros((number_of,), jnp.int32).at[order[jnp.where(places < fixed, places, moved)]].set(jnp.asarray(sizes, jnp.int32))

    sizes = jnp.where(number % 4 == 0, named(packed, number // 4), named(usual, number - number // 4 - 1))
    mixed = jax.random.permutation(jax.random.fold_in(own, 3), number_of)
    source_of, receiver = mixed[0:number_of // 2 * 2:2], mixed[1:number_of // 2 * 2:2]
    margin = jnp.minimum(sizes[source_of] - 1, reach - sizes[receiver]) // 2
    margin = jnp.where((source_of == order[0]) | (receiver == order[0]) | (sizes[receiver] == 0), 0, jnp.maximum(margin, 0))
    moved = jax.random.randint(jax.random.fold_in(own, 4), (number_of // 2,), 0, 1 << 20) % (margin + 1)
    sizes = sizes.at[source_of].add(-moved).at[receiver].add(moved)
    items = jnp.searchsorted(jnp.cumsum(sizes), jnp.arange(rows * top), side="right").astype(jnp.int32)
    grid = items.reshape(top, rows).T
    grid = grid[jax.random.permutation(jax.random.fold_in(own, 1), rows)]
    offset_by = jax.random.randint(jax.random.fold_in(own, 2), (rows, 1), 0, top)
    return jnp.take_along_axis(grid, (jnp.arange(top)[None, :] + offset_by) % top, axis=1)


def shares(count, total, reach, slope, full):
    loads = [(1 << 20) // math.isqrt(grade ** slope) + 1 for grade in range(1, count + 1)]
    largest = reach if full else min(reach, max(-(-total // count), total * loads[0] // sum(loads)))
    least = 1 if total - largest >= count - 1 else 0
    counts, spare = [largest] + [least] * (count - 1), total - largest - least * (count - 1)
    while spare > 0:
        free = [i for i in range(1, count) if counts[i] < largest] or [i for i in range(1, count) if counts[i] < reach]
        pool, left = sum([loads[i] for i in free]), spare
        for i in free:
            more = min(reach - counts[i], max(1, left * loads[i] // pool), spare)
            counts[i] = counts[i] + more
            spare = spare - more
    return np.array(counts)


def centred(rng, shape, spread, limit, cuts=(), held_as=jnp.bfloat16):
    factor_of = block_levels(rng, shape, cuts, -0.22, 0.18) if cuts else 1.0
    entries = jax.random.normal(rng, shape, jnp.float32) * spread * factor_of
    return jnp.minimum(jnp.maximum(entries, -limit), limit).astype(held_as)


def setup_inputs(seed: int = 0) -> dict:
    arg_keys = jax.random.split(jax.random.key(seed), 9)
    line_vectors = draw_line_vectors(jax.random.fold_in(arg_keys[8], 71), 0)
    mode_vectors = centred(arg_keys[1], (VECS, MODES), 1.0, 6.0, ((0, 8), (1, 64)), jnp.float32)
    line_diagonal = jnp.clip(2.0 + 2.0 * jax.random.uniform(arg_keys[2], (STATES,), jnp.float32) ** block_levels(arg_keys[2], (STATES,), ((0, 64),), -0.2, 0.2), 2.0, 4.0)
    line_links = jnp.clip(0.2 + 0.7 * jax.random.uniform(arg_keys[3], (STATES,), jnp.float32) ** block_levels(arg_keys[3], (STATES,), ((0, 64),), -0.2, 0.2), 0.2, 0.9)
    stiffness = jnp.clip(jnp.exp(math.log(6.0) - 2.4849066 * jax.random.uniform(arg_keys[4], (MODES,), jnp.float32) ** block_levels(arg_keys[4], (MODES,), ((0, 64),), -0.2, 0.2)), 0.5, 6.0)
    coupling_tiles = centred(arg_keys[5], (ATTACH, PANEL, MB), (8 * PANEL) ** -0.5, 0.1875, ((0, 64),))
    attachments_keys = jax.random.split(jax.random.fold_in(arg_keys[6], 1), ATTACH // ATT_DEV)
    attachments_turns = jax.random.permutation(jax.random.fold_in(arg_keys[6], 3), ATTACH // ATT_DEV)
    attachments = jax.vmap(lambda own, number: deal_out(jax.random.fold_in(arg_keys[6], 2), own, number, ATT_DEV, N_SEG, 1, CAP, 2))(attachments_keys, attachments_turns).reshape((ATTACH, 1))
    block_counts = jax.vmap(lambda own: ragged(own, SEG_DEV, ATT_DEV, A_MAX, 1))(jax.random.split(arg_keys[7], N_SEG)).reshape((N_SEG, SEG_DEV)).astype(jnp.int32)
    return {"line_vectors": line_vectors, "mode_vectors": mode_vectors, "line_diagonal": line_diagonal, "line_links": line_links, "stiffness": stiffness, "coupling_tiles": coupling_tiles, "attachments": attachments, "block_counts": block_counts}


center_shift = 3.0
half_width = 2.5


def layout(per_block, owners):
    attached = owners.shape[0]
    positions = jnp.arange(attached, dtype=jnp.int32)
    block_ends = jnp.cumsum(per_block).astype(jnp.int32)
    block_starts = block_ends - per_block
    block_of = jnp.sum((positions[:, None] >= block_ends[None, :]).astype(jnp.int32), 1)
    chosen = block_of[:, None] == jnp.arange(per_block.shape[0], dtype=jnp.int32)[None, :]
    first_slot = jnp.sum(jnp.where(chosen, block_starts[None, :], 0), 1).astype(jnp.int32)
    return (block_of * PANELS + positions - first_slot).astype(jnp.int32)


def operate(line_part, mode_part, line_diagonal, line_links, stiffness, coupling_tiles, attachments, block_counts):
    zero_column = jnp.zeros((VECS, 1), jnp.float32)
    line_next = jnp.concatenate([line_part[:, 1:], zero_column], 1)
    linked = line_links * line_part
    linked_prev = jnp.concatenate([zero_column, linked[:, :-1]], 1)
    acoustic = line_diagonal * line_part - line_links * line_next - linked_prev
    rounded_line = line_part.astype(jnp.bfloat16)
    mode_blocks = mode_part.astype(jnp.bfloat16).astype(jnp.float32).reshape(VECS, N_SEG, MB)
    owner_list = attachments[:, 0]

    def device_step(gathered_sum, device):
        owners = lax.dynamic_slice_in_dim(owner_list, device * ATT_DEV, ATT_DEV)
        panel_index = layout(block_counts[device], owners)
        line_rows = lax.dynamic_slice_in_dim(rounded_line, device * ROWS_DEV, ROWS_DEV, 1)
        line_rows = line_rows.reshape(VECS, SEG_DEV * PANELS, PANEL)
        panels = jnp.take(line_rows, panel_index, axis=1).astype(jnp.float32)
        tile_block = lax.dynamic_slice_in_dim(coupling_tiles, device * ATT_DEV, ATT_DEV, 0).astype(jnp.float32)
        outgoing = jnp.einsum('vtp,tpm->tvm', panels, tile_block).astype(jnp.bfloat16)
        outgoing = lax.optimization_barrier(outgoing).astype(jnp.float32)
        gathered_sum = gathered_sum.at[owners].add(outgoing)
        picked = jnp.take(mode_blocks, owners, axis=1)
        products = jnp.einsum('vtm,tpm->vtp', picked, tile_block)
        coupled = jnp.zeros((VECS, SEG_DEV * PANELS, PANEL), jnp.float32).at[:, panel_index, :].add(products)
        return gathered_sum, coupled.reshape(VECS, ROWS_DEV)

    gathered_sum, coupled_all = lax.scan(device_step, jnp.zeros((N_SEG, VECS, MB), jnp.float32), jnp.arange(N_SEG, dtype=jnp.int32))
    coupled_line = jnp.transpose(coupled_all, (1, 0, 2)).reshape(VECS, STATES)
    image_mode = stiffness * mode_part + jnp.transpose(gathered_sum, (1, 0, 2)).reshape(VECS, MODES)
    return acoustic + coupled_line, image_mode


def reference(line_vectors, mode_vectors, line_diagonal, line_links, stiffness, coupling_tiles, attachments, block_counts):
    extra = (line_diagonal, line_links, stiffness, coupling_tiles, attachments, block_counts)
    image_line, image_mode = operate(line_vectors, mode_vectors, *extra)
    first_line = (image_line - center_shift * line_vectors) / half_width
    first_mode = (image_mode - center_shift * mode_vectors) / half_width
    image_line, image_mode = operate(first_line, first_mode, *extra)
    filtered_line = 2.0 * (image_line - center_shift * first_line) / half_width - line_vectors
    filtered_modes = 2.0 * (image_mode - center_shift * first_mode) / half_width - mode_vectors
    rounded_line = filtered_line.astype(jnp.bfloat16)
    rounded_mode = filtered_modes.astype(jnp.bfloat16)
    summed_gram = jnp.dot(rounded_line, rounded_line.T, preferred_element_type=jnp.float32)
    summed_gram = summed_gram + jnp.dot(rounded_mode, rounded_mode.T, preferred_element_type=jnp.float32)
    gram_matrix = summed_gram / (STATES + MODES)
    return filtered_line, filtered_modes, gram_matrix
```

```python
import jax
import jax.numpy as jnp
from jax import lax
from jax.experimental import pallas as pl
from jax.experimental.pallas import tpu as pltpu
from jax.sharding import PartitionSpec as P

F32 = jnp.float32
BF16 = jnp.bfloat16
I32 = jnp.int32
PANEL = 128
PANELS = 24
SLOTS = 48
ATT = 44
COLS = 32
MB = 256
TOTAL = 393216 + 16384
MESH = pl.DeviceIdType.MESH
NT = (((1,), (1,)), ((), ()))

AG = (0, 16)
RS = (32, 48)
HALO = (64, 66)
GRAM = 72
MODE = 80
PLANE = 88
ZSUM = 120
LAST = 136
MESSAGES = 144


def tables_kernel(att, counts, tab):
    c0 = counts[0, 0]

    def clear(i, _):
        tab[i] = 0
        tab[64 + i] = 64
        tab[128 + i] = SLOTS
        tab[192 + i] = SLOTS
        return 0

    lax.fori_loop(0, 64, clear, 0, unroll=8)

    def one(t, _):
        slot = jnp.where(t < c0, t, t - c0 + PANELS)
        o = att[t, 0]
        z = o // 8
        pos = (z % 2) * 4 + (z // 2 % 2) * 2 + z // 4
        block = (o % 2) * 32 + (o // 2 % 4) * 8 + pos
        tab[slot] = t
        tab[64 + slot] = block
        first = tab[128 + block]
        free = first == SLOTS
        tab[192 + block] = jnp.where(free, SLOTS, slot)
        tab[128 + block] = jnp.where(free, slot, first)
        return 0

    lax.fori_loop(0, ATT, one, 0, unroll=4)


def kernel(
    tab, x_ref, y_ref, diag, links, stiff, tiles,
    line_out, mode_out, gram_out,
    g1, g2, out, s_buf, c_buf, r_buf, z_buf, xe, we, halo, w_mode, fb, gb, fm, mb, g_acc, p_buf, p_recv, q_buf, q_recv, last,
    send, recv,
):
    s = lax.axis_index("seg")
    v = lax.axis_index("vec")
    core, x, z = s % 2, s // 2 % 4, s // 8
    yy, zh = v // 2, v % 2
    pos = (z % 2) * 4 + (z // 2 % 2) * 2 + z // 4
    xr, xl, xo = (x + 1) % 4, (x + 3) % 4, (x + 2) % 4
    pc = 1 - core
    started = []

    def seg_of(zz, xx, cc):
        return zz * 8 + xx * 2 + cc

    def flip(a, n):
        return a + n - 2 * n * (a // n % 2)

    partner = seg_of(z, x, pc)
    right, left = seg_of(z, xr, core), seg_of(z, xl, core)
    z_peer = (seg_of(flip(z, 4), x, core), seg_of(flip(z, 2), x, core), seg_of(flip(z, 1), x, core))

    def copy(i, src, dst, seg, vec=None):
        return pltpu.make_async_remote_copy(
            src_ref=src, dst_ref=dst, send_sem=send.at[i], recv_sem=recv.at[i],
            device_id=(seg, v if vec is None else vec), device_id_type=MESH,
        )

    def go(i, src, dst, seg, vec=None):
        c = copy(i, src, dst, seg, vec)
        c.start()
        started.append(c)

    def got(i, dst):
        copy(i, dst, dst, partner).wait_recv()

    lane = lax.broadcasted_iota(I32, (COLS, PANEL), 1)

    def ag_start(r, g, mode):
        g[64] = jnp.zeros((COLS, MB), BF16)
        mine = core * 32 + x * 8 + pos
        g[mine] = mode.astype(BF16)
        go(AG[r], g.at[pl.ds(mine, 1)], g.at[pl.ds(mine, 1)], z_peer[0])

    def ag_z(r, g, step):
        have = (1, 2)[step]
        row = core * 32 + x * 8
        theirs = row + flip(pos // have * have, have)
        got(AG[r] + step, g.at[pl.ds(theirs, have)])
        run = row + pos // (2 * have) * (2 * have)
        go(AG[r] + step + 1, g.at[pl.ds(run, 2 * have)], g.at[pl.ds(run, 2 * have)], z_peer[step + 1])

    def ag_x(r, g):
        row = core * 32 + x * 8
        got(AG[r] + 2, g.at[pl.ds(row + 4 - pos // 4 * 4, 4)])
        mine = g.at[pl.ds(row, 8)]
        go(AG[r] + 3, mine, mine, right)
        go(AG[r] + 4, mine, mine, left)
        go(AG[r] + 7, mine, mine, partner)

    def ag_forward(r, g):
        from_left = g.at[pl.ds(core * 32 + xl * 8, 8)]
        got(AG[r] + 3, from_left)
        half = g.at[pl.ds(core * 32 + xl * 8, 4)]
        go(AG[r] + 5, half, half, right)
        go(AG[r] + 8, from_left, from_left, partner)
        from_right = g.at[pl.ds(core * 32 + xr * 8, 8)]
        got(AG[r] + 4, from_right)
        half = g.at[pl.ds(core * 32 + xr * 8 + 4, 4)]
        go(AG[r] + 6, half, half, left)
        go(AG[r] + 9, from_right, from_right, partner)

    def ag_opposite(r, g):
        for part in (0, 1):
            far = g.at[pl.ds(core * 32 + xo * 8 + part * 4, 4)]
            got(AG[r] + 5 + part, far)
            go(AG[r] + 10 + part, far, far, partner)

    def ag_end(r, g):
        for i, xx in ((7, x), (8, xl), (9, xr)):
            got(AG[r] + i, g.at[pl.ds(pc * 32 + xx * 8, 8)])
        for part in (0, 1):
            got(AG[r] + 10 + part, g.at[pl.ds(pc * 32 + xo * 8 + part * 4, 4)])

    def outgoing(src, low, high):
        def one(q, _):
            panel = src[q].astype(BF16)
            out[q] = jnp.dot(panel, tiles[tab[q]], preferred_element_type=F32).astype(BF16)
            return 0

        lax.fori_loop(low, high, one, 0, unroll=4)

    def sums(r, base):
        def one(i, _):
            b = base + i
            s_buf[r, b] = out[tab[128 + b]].astype(F32) + out[tab[192 + b]].astype(F32)
            return 0

        lax.fori_loop(0, 8, one, 0, unroll=4)

    def rs_core(r):
        for i, xx in enumerate((xo, xr, xl, x)):
            sums(r, pc * 32 + xx * 8)
            go(RS[r] + i, s_buf.at[r, pl.ds(pc * 32 + xx * 8, 8)], c_buf.at[r, pl.ds(xx * 8, 8)], partner)
        for xx in (xo, xr, xl, x):
            sums(r, core * 32 + xx * 8)

    def add(r, base, ref, start, n):
        def one(i, _):
            s_buf[r, base + i] = s_buf[r, base + i] + ref[r, start + i]
            return 0

        lax.fori_loop(0, n, one, 0, unroll=min(n, 4))

    def rs_x_first(r):
        for i, xx in enumerate((xo, xr, xl, x)):
            got(RS[r] + i, c_buf.at[r, pl.ds(xx * 8, 8)])
            base = core * 32 + xx * 8
            add(r, base, c_buf, xx * 8, 8)
            if i == 0:
                go(RS[r] + 4, s_buf.at[r, pl.ds(base, 4)], r_buf.at[r, pl.ds(0, 4)], right)
                go(RS[r] + 5, s_buf.at[r, pl.ds(base + 4, 4)], r_buf.at[r, pl.ds(4, 4)], left)
            if i == 1:
                go(RS[r] + 6, s_buf.at[r, pl.ds(base + 4, 4)], r_buf.at[r, pl.ds(12, 4)], right)
            if i == 2:
                go(RS[r] + 7, s_buf.at[r, pl.ds(base, 4)], r_buf.at[r, pl.ds(16, 4)], left)

    def rs_x_second(r):
        got(RS[r] + 4, r_buf.at[r, pl.ds(0, 4)])
        base = core * 32 + xr * 8
        add(r, base, r_buf, 0, 4)
        go(RS[r] + 8, s_buf.at[r, pl.ds(base, 4)], r_buf.at[r, pl.ds(8, 4)], right)
        got(RS[r] + 5, r_buf.at[r, pl.ds(4, 4)])
        base = core * 32 + xl * 8 + 4
        add(r, base, r_buf, 4, 4)
        go(RS[r] + 9, s_buf.at[r, pl.ds(base, 4)], r_buf.at[r, pl.ds(20, 4)], left)

    def rs_x_end(r):
        base = core * 32 + x * 8
        for i, at, half in ((6, 12, 4), (7, 16, 0), (8, 8, 0), (9, 20, 4)):
            got(RS[r] + i, r_buf.at[r, pl.ds(at, 4)])
            add(r, base + half, r_buf, at, 4)

    def rs_z_send(r, step):
        n, at = ((4, 0), (2, 4), (1, 6))[step]
        run = core * 32 + x * 8 + flip(pos // n * n, n)
        go(RS[r] + 10 + step, s_buf.at[r, pl.ds(run, n)], z_buf.at[r, pl.ds(at, n)], z_peer[2 - step])

    def rs_z_add(r, step):
        n, at = ((4, 0), (2, 4), (1, 6))[step]
        got(RS[r] + 10 + step, z_buf.at[r, pl.ds(at, n)])
        add(r, core * 32 + x * 8 + pos // n * n, z_buf, at, n)

    def halo_send(r, src):
        halo[r, 2] = src[SLOTS - 1] * links[pl.ds(SLOTS - 1, 1), :]
        go(HALO[r], src.at[0], halo.at[r, 0], (s + 63) % 64)
        go(HALO[r] + 1, halo.at[r, 2], halo.at[r, 1], (s + 1) % 64)

    def halo_take(r, src):
        got(HALO[r], halo.at[r, 0])
        got(HALO[r] + 1, halo.at[r, 1])
        src[SLOTS] = jnp.where(s < 63, halo[r, 0], 0.0)
        halo[r, 3] = jnp.where(s > 0, halo[r, 1], 0.0)

    def shifted(r, src, g, q, before):
        here = src[q]
        link = links[pl.ds(q, 1), :]
        linked = link * here
        after = jnp.where(lane == PANEL - 1, pltpu.roll(src[q + 1], PANEL - 1, 1), pltpu.roll(here, PANEL - 1, 1))
        prior = jnp.where(lane == 0, pltpu.roll(before, 1, 1), pltpu.roll(linked, 1, 1))
        coupled = lax.dot_general(g[tab[64 + q]], tiles[tab[q]], NT, preferred_element_type=F32)
        return (diag[pl.ds(q, 1), :] - 3.0) * here - link * after - prior + coupled, linked

    def stiffened(mode):
        wide = jnp.concatenate([stiff[pl.ds(0, 1), :], stiff[pl.ds(1, 1), :]], 1) - 3.0
        return wide * mode

    for q in range(SLOTS):
        xe[q] = x_ref[:, q * PANEL : (q + 1) * PANEL]
    out[SLOTS] = jnp.zeros((COLS, MB), BF16)
    ag_start(0, g1, y_ref[...])
    halo_send(0, xe)
    outgoing(xe, 0, 16)
    ag_z(0, g1, 0)
    outgoing(xe, 16, 32)
    ag_z(0, g1, 1)
    outgoing(xe, 32, 48)
    rs_core(0)
    ag_x(0, g1)
    rs_x_first(0)
    ag_forward(0, g1)
    rs_x_second(0)
    ag_opposite(0, g1)
    halo_take(0, xe)
    ag_end(0, g1)

    def first_panel(q, before):
        image, linked = shifted(0, xe, g1, q, before)
        we[q] = image * 0.4
        return linked

    lax.fori_loop(0, SLOTS, first_panel, halo[0, 3], unroll=4)
    halo_send(1, we)
    rs_x_end(0)
    rs_z_send(0, 0)
    outgoing(we, 0, 24)
    rs_z_add(0, 0)
    rs_z_send(0, 1)
    outgoing(we, 24, 48)
    rs_z_add(0, 1)
    rs_z_send(0, 2)
    rs_core(1)
    rs_z_add(0, 2)
    w_mode[...] = (stiffened(y_ref[...]) + s_buf[0, core * 32 + x * 8 + pos]) * 0.4

    ag_start(1, g2, w_mode[...])
    rs_x_first(1)
    ag_z(1, g2, 0)
    ag_z(1, g2, 1)
    ag_x(1, g2)
    rs_x_second(1)
    ag_forward(1, g2)
    halo_take(1, we)
    ag_opposite(1, g2)
    rs_x_end(1)
    rs_z_send(1, 0)
    ag_end(1, g2)

    def second_panel(q, before):
        image, linked = shifted(1, we, g2, q, before)
        value = image * 0.8 - xe[q]
        line_out[:, pl.ds(pl.multiple_of(q * PANEL, PANEL), PANEL)] = value
        fb[q] = value.astype(BF16)
        return linked

    far_first = ((0, 1), (1, 1), (2, 1), (3, 1), (1, 0), (2, 0), (3, 0), (0, 0))
    for dy, dz in far_first:
        k = (yy + dy) % 4 * 2 + (zh + dz) % 2
        q0 = k * 6
        ahead = jnp.maximum(q0 - 1, 0)
        before = jnp.where(q0 > 0, links[pl.ds(ahead, 1), :] * we[ahead], halo[1, 3])
        lax.fori_loop(0, 6, lambda i, b, q0=q0: second_panel(q0 + i, b), before, unroll=3)
        if (dy, dz) != (0, 0):
            go(GRAM + dy * 2 + dz, fb.at[pl.ds(q0, 6)], gb.at[v], s, k)

    rs_z_add(1, 0)
    rs_z_send(1, 1)
    gb[v] = fb[pl.ds(v * 6, 6)]
    rs_z_add(1, 1)
    rs_z_send(1, 2)
    rs_z_add(1, 2)
    filtered = (stiffened(w_mode[...]) + s_buf[1, core * 32 + x * 8 + pos]) * 0.8 - y_ref[...]
    mode_out[...] = filtered
    fm[...] = filtered.astype(BF16)

    keeper = s % 8

    def mode_number(one, other):
        return MODE + (one // 2 - other // 2 + 4) % 4 * 2 + (one + other) % 2

    @pl.when(v != keeper)
    def _():
        copy(mode_number(keeper, v), fm, mb.at[v], s, keeper).start()

    @pl.when(v == keeper)
    def _():
        mb[v] = fm[...]

    for dy, dz in far_first[4:7] + far_first[:4]:
        frm = (yy + 4 - dy) % 4 * 2 + (zh + dz) % 2
        got(GRAM + dy * 2 + dz, gb.at[frm])
    wide = jnp.concatenate([gb[:, p].reshape(8 * COLS, PANEL) for p in range(6)], 1)
    g_acc[...] = lax.dot_general(wide, wide, NT, preferred_element_type=F32)

    @pl.when(v != keeper)
    def _():
        copy(mode_number(keeper, v), fm, mb.at[v], s, keeper).wait_send()

    @pl.when(v == keeper)
    def _():
        for dy, dz in far_first[:7]:
            frm = (yy + 4 - dy) % 4 * 2 + (zh + dz) % 2
            got(MODE + dy * 2 + dz, mb.at[frm])
        modes = mb[...].reshape(8 * COLS, MB)
        g_acc[...] += lax.dot_general(modes, modes, NT, preferred_element_type=F32)

    for y1 in range(4):
        for x1 in range(4):
            for c1 in range(2):
                for h1 in range(2):
                    row = (y1 * 2 + h1) * 32 + x1 * 8
                    p_buf[(y1 * 4 + x1) * 2 + c1, h1] = g_acc[row : row + 8, c1 * 128 : c1 * 128 + 128]

    def plane_copy(r):
        w1 = (yy + r // 8) % 4, (x + r // 2 % 4) % 4, (core + r % 2) % 2
        src = p_buf.at[(w1[0] * 4 + w1[1]) * 2 + w1[2]]
        return copy(PLANE + r, src, p_recv.at[r], seg_of(z, w1[1], w1[2]), w1[0] * 2 + zh)

    def start_plane(r, _):
        plane_copy(r).start()
        return 0

    lax.fori_loop(1, 32, start_plane, 0)

    def take_plane(r, total):
        got(PLANE + r, p_recv.at[r])
        return total + p_recv[r]

    mine = (yy * 4 + x) * 2 + core
    q_buf[...] = lax.fori_loop(1, 32, take_plane, p_buf[mine])

    def z_copy(r):
        u = (zh * 8 + z + r) % 16
        return copy(ZSUM + r, q_buf.at[u // 8], q_recv.at[r], seg_of(u % 8, x, core), yy * 2 + u // 8)

    def start_z(r, _):
        z_copy(r).start()
        return 0

    lax.fori_loop(1, 16, start_z, 0)

    def take_z(r, total):
        got(ZSUM + r, q_recv.at[r])
        return total + q_recv[r]

    j = x * 2 + core
    last[j] = lax.fori_loop(1, 16, take_z, q_buf[zh]) * (1.0 / TOTAL)

    def last_copy(r):
        j1 = (j + r) % 8
        return copy(LAST + r, last.at[j], last.at[j], seg_of(z, j1 // 2, j1 % 2))

    for r in range(1, 8):
        last_copy(r).start()
    for r in range(1, 8):
        got(LAST + r, last.at[(j + 8 - r) % 8])
    for j1 in range(8):
        gram_out[j1 // 2 * 8 : j1 // 2 * 8 + 8, j1 % 2 * 128 : j1 % 2 * 128 + 128] = last[j1]

    for c in started:
        c.wait_send()

    def end_plane(r, _):
        plane_copy(r).wait_send()
        return 0

    lax.fori_loop(1, 32, end_plane, 0)

    def end_z(r, _):
        z_copy(r).wait_send()
        return 0

    lax.fori_loop(1, 16, end_z, 0)
    for r in range(1, 8):
        last_copy(r).wait_send()


def body(line_vectors, mode_vectors, line_diagonal, line_links, stiffness, coupling_tiles, attachments, block_counts):
    tab = pl.pallas_call(
        tables_kernel,
        out_shape=jax.ShapeDtypeStruct((256,), I32),
        in_specs=[pl.BlockSpec(memory_space=pltpu.SMEM)] * 2,
        out_specs=pl.BlockSpec(memory_space=pltpu.SMEM),
    )(attachments, block_counts)
    block = (COLS, MB)
    return pl.pallas_call(
        kernel,
        out_shape=(
            jax.ShapeDtypeStruct((COLS, SLOTS * PANEL), F32),
            jax.ShapeDtypeStruct(block, F32),
            jax.ShapeDtypeStruct((COLS, 8 * COLS), F32),
        ),
        in_specs=[pl.BlockSpec(memory_space=pltpu.SMEM)] + [pl.BlockSpec(memory_space=pltpu.VMEM)] * 6,
        out_specs=[pl.BlockSpec(memory_space=pltpu.VMEM)] * 3,
        scratch_shapes=[
            pltpu.VMEM((65,) + block, BF16),
            pltpu.VMEM((65,) + block, BF16),
            pltpu.VMEM((SLOTS + 1,) + block, BF16),
            pltpu.VMEM((2, 64) + block, F32),
            pltpu.VMEM((2, 32) + block, F32),
            pltpu.VMEM((2, 24) + block, F32),
            pltpu.VMEM((2, 7) + block, F32),
            pltpu.VMEM((SLOTS + 1, COLS, PANEL), F32),
            pltpu.VMEM((SLOTS + 1, COLS, PANEL), F32),
            pltpu.VMEM((2, 4, COLS, PANEL), F32),
            pltpu.VMEM(block, F32),
            pltpu.VMEM((SLOTS, COLS, PANEL), BF16),
            pltpu.VMEM((8, 6, COLS, PANEL), BF16),
            pltpu.VMEM(block, BF16),
            pltpu.VMEM((8,) + block, BF16),
            pltpu.VMEM((256, 256), F32),
            pltpu.VMEM((32, 2, 8, 128), F32),
            pltpu.VMEM((32, 2, 8, 128), F32),
            pltpu.VMEM((2, 8, 128), F32),
            pltpu.VMEM((16, 8, 128), F32),
            pltpu.VMEM((8, 8, 128), F32),
            pltpu.SemaphoreType.DMA((MESSAGES,)),
            pltpu.SemaphoreType.DMA((MESSAGES,)),
        ],
        compiler_params=pltpu.CompilerParams(has_side_effects=True, vmem_limit_bytes=50 * 2**20),
    )(
        tab,
        line_vectors,
        mode_vectors,
        line_diagonal.reshape(SLOTS, PANEL),
        line_links.reshape(SLOTS, PANEL),
        stiffness.reshape(2, PANEL),
        coupling_tiles,
    )


def solution(mesh):
    in_specs = (
        P("vec", "seg"),
        P("vec", "seg"),
        P("seg"),
        P("seg"),
        P("seg"),
        P("seg", None, None),
        P("seg", None),
        P("seg", None),
    )
    out_specs = (P("vec", "seg"), P("vec", "seg"), P("vec", None))
    return jax.shard_map(body, mesh=mesh, in_specs=in_specs, out_specs=out_specs, check_vma=False)
```

```python
import jax
import jax.numpy as jnp
from jax import lax
from jax.experimental import pallas as pl
from jax.experimental.pallas import tpu as pltpu
from jax.sharding import PartitionSpec as P

F32 = jnp.float32
BF16 = jnp.bfloat16
I32 = jnp.int32
PANEL = 128
PANELS = 24
SLOTS = 48
ATT = 44
COLS = 32
MB = 256
TOTAL = 393216 + 16384
MESH = pl.DeviceIdType.MESH
NT = (((1,), (1,)), ((), ()))

AG = (0, 24)
RS = (48, 88)
HALO = (128, 130)
GRAM = 136
MODE = 144
PLANE = 152
ZSUM = 184
LAST = 200
MESSAGES = 208
FAR = (4, 5, 6, 7, 2, 3, 1, 0)


def kernel(
    att, counts, x_hbm, y_hbm, diag_hbm, links_hbm, stiff_hbm, tiles_hbm, att_hbm,
    line_out, mode_out, gram_out,
    x_ref, y_ref, diag, links, stiff, tiles, owner_row, tab_v, tab,
    g1, g2, out, s_buf, c_buf, r_buf, z_buf, xe, we, halo, w_mode, fb, gb, fm, mb, g_acc, p_buf, p_recv, q_buf, q_recv, last,
    send, recv, load,
):
    s = lax.axis_index("seg")
    v = lax.axis_index("vec")
    core, x, z = s % 2, s // 2 % 4, s // 8
    yy, zh = v // 2, v % 2
    pc = 1 - core
    started = []

    def seg_of(zz, xx, cc):
        return zz * 8 + xx * 2 + cc

    def flip(a, n):
        for bit in (1, 2, 4):
            if n & bit:
                a = a + bit - 2 * bit * (a // bit % 2)
        return a

    partner = seg_of(z, x, pc)
    x_of = [(x + d) % 4 for d in range(4)]
    z_of = [flip(z, k) for k in range(8)]
    far_first = ((0, 1), (1, 1), (2, 1), (3, 1), (1, 0), (2, 0), (3, 0), (0, 0))

    barrier = pltpu.get_barrier_semaphore()
    peers = [(partner, v), ((s + 1) % 64, v), ((s + 63) % 64, v)]
    peers += [(seg_of(z, x_of[d], core), v) for d in (1, 2, 3)]
    peers += [(seg_of(z_of[k], x, core), v) for k in range(1, 8)]
    peers += [(s, (yy + dy) % 4 * 2 + (zh + dz) % 2) for dy, dz in far_first[:7]]
    for peer in peers:
        pl.semaphore_signal(barrier, inc=1, device_id=peer, device_id_type=MESH)

    pairs = [(x_hbm, x_ref), (y_hbm, y_ref), (diag_hbm, diag), (links_hbm, links), (stiff_hbm, stiff), (att_hbm, owner_row)]
    pairs += [(tiles_hbm.at[pl.ds(i * 11, 11)], tiles.at[pl.ds(i * 11, 11)]) for i in range(4)]
    loads = [pltpu.make_async_copy(a, b, load.at[i]) for i, (a, b) in enumerate(pairs)]
    for i in (5, 0, 6, 7, 8, 9, 1, 2, 3, 4):
        loads[i].start()

    def copy(i, src, dst, seg, vec=None):
        return pltpu.make_async_remote_copy(
            src_ref=src, dst_ref=dst, send_sem=send.at[i], recv_sem=recv.at[i],
            device_id=(seg, v if vec is None else vec), device_id_type=MESH,
        )

    def go(i, src, dst, seg, vec=None):
        c = copy(i, src, dst, seg, vec)
        c.start()
        started.append(c)

    def got(i, dst):
        copy(i, dst, dst, partner).wait_recv()

    lane = lax.broadcasted_iota(I32, (COLS, PANEL), 1)
    c0 = counts[0, 0]

    def block_of(owner):
        return owner % 2 * 32 + owner // 2 % 4 * 8 + owner // 8

    runs = ((z // 2 * 2, 2), (flip(z, 2) // 2 * 2, 2), (flip(z, 4) // 4 * 4, 4))

    def ag_start(r, g, mode):
        g[64] = jnp.zeros((COLS, MB), BF16)
        mine = core * 32 + x * 8 + z
        g[mine] = mode.astype(BF16)
        for k in (7, 6, 5, 4, 3, 2, 1):
            go(AG[r] + k, g.at[mine], g.at[mine], seg_of(z_of[k], x, core))

    def ag_x(r, g, piece):
        for k in ((1,), (2, 3), (4, 5, 6, 7))[piece]:
            got(AG[r] + k, g.at[core * 32 + x * 8 + z_of[k]])
        run = g.at[pl.ds(core * 32 + x * 8 + runs[piece][0], runs[piece][1])]
        for d in (2, 1, 3):
            go(AG[r] + 8 + piece * 3 + d - 1, run, run, seg_of(z, x_of[d], core))

    def ag_core(r, g):
        for d in (0, 1, 3, 2):
            row = core * 32 + x_of[-d % 4] * 8
            for piece in range(3) if d else ():
                got(AG[r] + 8 + piece * 3 + d - 1, g.at[pl.ds(row + runs[piece][0], runs[piece][1])])
            whole = g.at[pl.ds(row, 8)]
            go(AG[r] + 17 + d, whole, whole, partner)

    def ag_end(r, g):
        for d in (0, 1, 3, 2):
            got(AG[r] + 17 + d, g.at[pl.ds(pc * 32 + x_of[-d % 4] * 8, 8)])

    def outgoing(src, low, high):
        def one(t, _):
            slot = jnp.minimum(jnp.where(t < c0, t, t - c0 + PANELS), SLOTS - 1)
            out[t] = jnp.dot(src[slot].astype(BF16), tiles[t], preferred_element_type=F32).astype(BF16)
            return 0

        lax.fori_loop(low, high, one, 0, unroll=4 if high - low == 44 else high - low)

    def sums(r, cc, k):
        def one(xx, _):
            b = cc * 32 + xx * 8 + z_of[k]
            s_buf[r, cc, xx, z_of[k]] = out[tab[0, b, 0]].astype(F32) + out[tab[1, b, 0]].astype(F32)
            return 0

        lax.fori_loop(0, 4, one, 0, unroll=True)

    def rs_core(r, k):
        go(RS[r] + k, s_buf.at[r, pc, :, z_of[k]], c_buf.at[r, :, z_of[k]], partner)

    def rs_x(r, k):
        zk = z_of[k]
        got(RS[r] + k, c_buf.at[r, :, zk])
        for xx in range(4):
            s_buf[r, core, xx, zk] = s_buf[r, core, xx, zk] + c_buf[r, xx, zk]
        for d in (2, 1, 3):
            go(RS[r] + 8 + k * 3 + d - 1, s_buf.at[r, core, x_of[d], zk], r_buf.at[r, d - 1, k], seg_of(z, x_of[d], core))

    def rs_z(r, k):
        zk = z_of[k]
        for d in (1, 2, 3):
            got(RS[r] + 8 + k * 3 + d - 1, r_buf.at[r, d - 1, k])
        s_buf[r, core, x, zk] = s_buf[r, core, x, zk] + r_buf[r, 0, k] + r_buf[r, 1, k] + r_buf[r, 2, k]
        if k:
            go(RS[r] + 32 + k, s_buf.at[r, core, x, zk], z_buf.at[r, k], seg_of(zk, x, core))

    def rs_end(r):
        total = s_buf[r, core, x, z]
        for k in range(1, 8):
            got(RS[r] + 32 + k, z_buf.at[r, k])
            total = total + z_buf[r, k]
        return total

    def halo_send(r, src):
        halo[r, 2] = src[SLOTS - 1] * links[pl.ds(SLOTS - 1, 1), :]
        go(HALO[r], src.at[0], halo.at[r, 0], (s + 63) % 64)
        go(HALO[r] + 1, halo.at[r, 2], halo.at[r, 1], (s + 1) % 64)

    def halo_take(r, src):
        got(HALO[r], halo.at[r, 0])
        got(HALO[r] + 1, halo.at[r, 1])
        src[SLOTS] = jnp.where(s < 63, halo[r, 0], 0.0)
        halo[r, 3] = jnp.where(s > 0, halo[r, 1], 0.0)

    def shifted(r, src, g, q, before):
        here = src[q]
        link = links[pl.ds(q, 1), :]
        linked = link * here
        after = jnp.where(lane == PANEL - 1, pltpu.roll(src[q + 1], PANEL - 1, 1), pltpu.roll(here, PANEL - 1, 1))
        prior = jnp.where(lane == 0, pltpu.roll(before, 1, 1), pltpu.roll(linked, 1, 1))
        second = q >= PANELS
        rank = jnp.where(second, q - PANELS, q)
        t = jnp.minimum(jnp.where(second, rank + c0, rank), ATT - 1)
        used = rank < jnp.where(second, counts[0, 1], c0)
        block = jnp.where(used, block_of(att[0, t]), 64)
        coupled = lax.dot_general(g[block], tiles[t], NT, preferred_element_type=F32)
        return (diag[pl.ds(q, 1), :] - 3.0) * here - link * after - prior + coupled, linked

    def stiffened(mode):
        wide = jnp.concatenate([stiff[pl.ds(0, 1), :], stiff[pl.ds(1, 1), :]], 1) - 3.0
        return wide * mode

    loads[5].wait()
    owner = owner_row[...]
    at = lax.broadcasted_iota(I32, (64, ATT), 1)
    same = jnp.broadcast_to(block_of(owner), (64, ATT)) == lax.broadcasted_iota(I32, (64, ATT), 0)
    one = jnp.min(jnp.where(same, at, ATT), 1, keepdims=True)
    two = jnp.max(jnp.where(same, at, -1), 1, keepdims=True)
    tab_v[0] = jnp.broadcast_to(one, (64, 128))
    tab_v[1] = jnp.broadcast_to(jnp.where(two > one, two, ATT), (64, 128))
    to_scalars = pltpu.make_async_copy(tab_v, tab, load.at[10])
    to_scalars.start()
    out[ATT] = jnp.zeros((COLS, MB), BF16)
    loads[0].wait()
    for q in range(SLOTS):
        xe[q] = x_ref[:, q * PANEL : (q + 1) * PANEL]
    for i in range(4):
        loads[6 + i].wait()
        outgoing(xe, i * 11, i * 11 + 11)
    to_scalars.wait()
    for i in range(1, 5):
        loads[i].wait()
    for k in FAR:
        sums(0, pc, k)
        sums(0, core, k)
    pl.semaphore_wait(barrier, len(peers))
    for k in FAR[:2]:
        rs_core(0, k)
    ag_start(0, g1, y_ref[...])
    for k in FAR[2:]:
        rs_core(0, k)
    for k in FAR:
        rs_x(0, k)
    halo_send(0, xe)
    for k in FAR[:2]:
        rs_z(0, k)
    ag_x(0, g1, 0)
    ag_x(0, g1, 1)
    for k in FAR[2:4]:
        rs_z(0, k)
    ag_x(0, g1, 2)
    for k in FAR[4:]:
        rs_z(0, k)
    ag_core(0, g1)
    halo_take(0, xe)
    ag_end(0, g1)

    def first_panel(q, before):
        image, linked = shifted(0, xe, g1, q, before)
        we[q] = image * 0.4
        return linked

    lax.fori_loop(0, SLOTS, first_panel, halo[0, 3], unroll=4)
    halo_send(1, we)
    w_mode[...] = (stiffened(y_ref[...]) + rs_end(0)) * 0.4

    ag_start(1, g2, w_mode[...])
    outgoing(we, 0, 44)
    for k in FAR:
        sums(1, pc, k)
        rs_core(1, k)
    for k in FAR:
        sums(1, core, k)
    for k in FAR[:2]:
        rs_x(1, k)
    for piece in range(3):
        ag_x(1, g2, piece)
    for k in FAR[2:]:
        rs_x(1, k)
    for k in FAR[:2]:
        rs_z(1, k)
    halo_take(1, we)
    ag_core(1, g2)
    for k in FAR[2:4]:
        rs_z(1, k)
    ag_end(1, g2)

    def second_panel(q, before):
        image, linked = shifted(1, we, g2, q, before)
        value = image * 0.8 - xe[q]
        line_out[:, pl.ds(pl.multiple_of(q * PANEL, PANEL), PANEL)] = value
        fb[q] = value.astype(BF16)
        return linked

    for dy, dz in far_first:
        k = (yy + dy) % 4 * 2 + (zh + dz) % 2
        q0 = k * 6
        ahead = jnp.maximum(q0 - 1, 0)
        before = jnp.where(q0 > 0, links[pl.ds(ahead, 1), :] * we[ahead], halo[1, 3])
        lax.fori_loop(0, 6, lambda i, b, q0=q0: second_panel(q0 + i, b), before, unroll=3)
        if (dy, dz) != (0, 0):
            go(GRAM + dy * 2 + dz, fb.at[pl.ds(q0, 6)], gb.at[v], s, k)

    gb[v] = fb[pl.ds(v * 6, 6)]
    for k in FAR[4:]:
        rs_z(1, k)
    filtered = (stiffened(w_mode[...]) + rs_end(1)) * 0.8 - y_ref[...]
    mode_out[...] = filtered
    fm[...] = filtered.astype(BF16)

    keeper = s % 8

    def mode_number(one, other):
        return MODE + (one // 2 - other // 2 + 4) % 4 * 2 + (one + other) % 2

    @pl.when(v != keeper)
    def _():
        copy(mode_number(keeper, v), fm, mb.at[v], s, keeper).start()

    @pl.when(v == keeper)
    def _():
        mb[v] = fm[...]

    for dy, dz in far_first[4:7] + far_first[:4]:
        frm = (yy + 4 - dy) % 4 * 2 + (zh + dz) % 2
        got(GRAM + dy * 2 + dz, gb.at[frm])
    wide = jnp.concatenate([gb[:, p].reshape(8 * COLS, PANEL) for p in range(6)], 1)
    g_acc[...] = lax.dot_general(wide, wide, NT, preferred_element_type=F32)

    @pl.when(v != keeper)
    def _():
        copy(mode_number(keeper, v), fm, mb.at[v], s, keeper).wait_send()

    @pl.when(v == keeper)
    def _():
        for dy, dz in far_first[:7]:
            frm = (yy + 4 - dy) % 4 * 2 + (zh + dz) % 2
            got(MODE + dy * 2 + dz, mb.at[frm])
        modes = mb[...].reshape(8 * COLS, MB)
        g_acc[...] += lax.dot_general(modes, modes, NT, preferred_element_type=F32)

    for y1 in range(4):
        for x1 in range(4):
            for c1 in range(2):
                for h1 in range(2):
                    row = (y1 * 2 + h1) * 32 + x1 * 8
                    p_buf[(y1 * 4 + x1) * 2 + c1, h1] = g_acc[row : row + 8, c1 * 128 : c1 * 128 + 128]

    def plane_copy(r):
        w1 = (yy + r // 8) % 4, (x + r // 2 % 4) % 4, (core + r % 2) % 2
        src = p_buf.at[(w1[0] * 4 + w1[1]) * 2 + w1[2]]
        return copy(PLANE + r, src, p_recv.at[r], seg_of(z, w1[1], w1[2]), w1[0] * 2 + zh)

    def start_plane(r, _):
        plane_copy(r).start()
        return 0

    lax.fori_loop(1, 32, start_plane, 0)

    def take_plane(r, total):
        got(PLANE + r, p_recv.at[r])
        return total + p_recv[r]

    mine = (yy * 4 + x) * 2 + core
    q_buf[...] = lax.fori_loop(1, 32, take_plane, p_buf[mine])

    def z_copy(r):
        u = (zh * 8 + z + r) % 16
        return copy(ZSUM + r, q_buf.at[u // 8], q_recv.at[r], seg_of(u % 8, x, core), yy * 2 + u // 8)

    def start_z(r, _):
        z_copy(r).start()
        return 0

    lax.fori_loop(1, 16, start_z, 0)

    def take_z(r, total):
        got(ZSUM + r, q_recv.at[r])
        return total + q_recv[r]

    j = x * 2 + core
    last[j] = lax.fori_loop(1, 16, take_z, q_buf[zh]) * (1.0 / TOTAL)

    def last_copy(r):
        j1 = (j + r) % 8
        return copy(LAST + r, last.at[j], last.at[j], seg_of(z, j1 // 2, j1 % 2))

    for r in range(1, 8):
        last_copy(r).start()
    for r in range(1, 8):
        got(LAST + r, last.at[(j + 8 - r) % 8])
    for j1 in range(8):
        gram_out[j1 // 2 * 8 : j1 // 2 * 8 + 8, j1 % 2 * 128 : j1 % 2 * 128 + 128] = last[j1]

    for c in started:
        c.wait_send()

    def end_plane(r, _):
        plane_copy(r).wait_send()
        return 0

    lax.fori_loop(1, 32, end_plane, 0)

    def end_z(r, _):
        z_copy(r).wait_send()
        return 0

    lax.fori_loop(1, 16, end_z, 0)
    for r in range(1, 8):
        last_copy(r).wait_send()


def body(line_vectors, mode_vectors, line_diagonal, line_links, stiffness, coupling_tiles, attachments, block_counts):
    block = (COLS, MB)
    owners = attachments.reshape(1, ATT)
    return pl.pallas_call(
        kernel,
        out_shape=(
            jax.ShapeDtypeStruct((COLS, SLOTS * PANEL), F32),
            jax.ShapeDtypeStruct(block, F32),
            jax.ShapeDtypeStruct((COLS, 8 * COLS), F32),
        ),
        in_specs=[pl.BlockSpec(memory_space=pltpu.SMEM)] * 2 + [pl.BlockSpec(memory_space=pltpu.HBM)] * 7,
        out_specs=[pl.BlockSpec(memory_space=pltpu.VMEM)] * 3,
        scratch_shapes=[
            pltpu.VMEM((COLS, SLOTS * PANEL), F32),
            pltpu.VMEM(block, F32),
            pltpu.VMEM((SLOTS, PANEL), F32),
            pltpu.VMEM((SLOTS, PANEL), F32),
            pltpu.VMEM((2, PANEL), F32),
            pltpu.VMEM((ATT, PANEL, MB), BF16),
            pltpu.VMEM((1, ATT), I32),
            pltpu.VMEM((2, 64, 128), I32),
            pltpu.SMEM((2, 64, 128), I32),
            pltpu.VMEM((65,) + block, BF16),
            pltpu.VMEM((65,) + block, BF16),
            pltpu.VMEM((ATT + 1,) + block, BF16),
            pltpu.VMEM((2, 2, 4, 8) + block, F32),
            pltpu.VMEM((2, 4, 8) + block, F32),
            pltpu.VMEM((2, 3, 8) + block, F32),
            pltpu.VMEM((2, 8) + block, F32),
            pltpu.VMEM((SLOTS + 1, COLS, PANEL), F32),
            pltpu.VMEM((SLOTS + 1, COLS, PANEL), F32),
            pltpu.VMEM((2, 4, COLS, PANEL), F32),
            pltpu.VMEM(block, F32),
            pltpu.VMEM((SLOTS, COLS, PANEL), BF16),
            pltpu.VMEM((8, 6, COLS, PANEL), BF16),
            pltpu.VMEM(block, BF16),
            pltpu.VMEM((8,) + block, BF16),
            pltpu.VMEM((256, 256), F32),
            pltpu.VMEM((32, 2, 8, 128), F32),
            pltpu.VMEM((32, 2, 8, 128), F32),
            pltpu.VMEM((2, 8, 128), F32),
            pltpu.VMEM((16, 8, 128), F32),
            pltpu.VMEM((8, 8, 128), F32),
            pltpu.SemaphoreType.DMA((MESSAGES,)),
            pltpu.SemaphoreType.DMA((MESSAGES,)),
            pltpu.SemaphoreType.DMA((11,)),
        ],
        compiler_params=pltpu.CompilerParams(
            has_side_effects=True, collective_id=0, vmem_limit_bytes=64 * 2**20
        ),
    )(
        owners,
        block_counts,
        line_vectors,
        mode_vectors,
        line_diagonal.reshape(SLOTS, PANEL),
        line_links.reshape(SLOTS, PANEL),
        stiffness.reshape(2, PANEL),
        coupling_tiles,
        owners,
    )


def solution(mesh):
    in_specs = (
        P("vec", "seg"),
        P("vec", "seg"),
        P("seg"),
        P("seg"),
        P("seg"),
        P("seg", None, None),
        P("seg", None),
        P("seg", None),
    )
    out_specs = (P("vec", "seg"), P("vec", "seg"), P("vec", None))
    return jax.shard_map(body, mesh=mesh, in_specs=in_specs, out_specs=out_specs, check_vma=False)
```

```python
import jax
import jax.numpy as jnp
from jax import lax
from jax.experimental import pallas as pl
from jax.experimental.pallas import tpu as pltpu
from jax.sharding import PartitionSpec as P

F32 = jnp.float32
BF16 = jnp.bfloat16
I32 = jnp.int32
PANEL = 128
PANELS = 24
SLOTS = 48
ATT = 44
COLS = 32
MB = 256
TOTAL = 393216 + 16384
MESH = pl.DeviceIdType.MESH
NT = (((1,), (1,)), ((), ()))

AG = (0, 24)
RS = (48, 96)
HALO = (144, 146)
GRAM = 152
MODE = 160
PLANE = 168
ZSUM = 200
LAST = 216
MESSAGES = 224
ORDER = (7, 6, 5, 4, 3, 2, 1, 0)


def kernel(
    att, counts, x_hbm, y_hbm, diag_hbm, links_hbm, stiff_hbm, tiles_hbm, att_hbm,
    line_out, mode_out, gram_out,
    x_ref, y_ref, diag, links, stiff, tiles, owner_row, tab_v, tab,
    g1, g2, out, s_buf, c_buf, r_buf, z_buf, xe, we, halo, w_mode, fb, gb, fm, mb, g_acc, p_buf, p_recv, q_buf, q_recv, last,
    send, recv, load,
):
    s = lax.axis_index("seg")
    v = lax.axis_index("vec")
    core, x, z = s % 2, s // 2 % 4, s // 8
    yy, zh = v // 2, v % 2
    pc = 1 - core
    started = []

    def seg_of(zz, xx, cc):
        return zz * 8 + xx * 2 + cc

    def flip(a, n):
        for bit in (1, 2, 4):
            if n & bit:
                a = a + bit - 2 * bit * (a // bit % 2)
        return a

    partner = seg_of(z, x, pc)
    x_of = [(x + d) % 4 for d in range(4)]
    z_of = [flip(z, k) for k in range(8)]
    far_first = ((0, 1), (1, 1), (2, 1), (3, 1), (1, 0), (2, 0), (3, 0), (0, 0))

    barrier = pltpu.get_barrier_semaphore()
    peers = [(partner, v), ((s + 1) % 64, v), ((s + 63) % 64, v)]
    peers += [(seg_of(z, x_of[d], core), v) for d in (1, 2, 3)]
    peers += [(seg_of(z_of[k], x, core), v) for k in range(1, 8)]
    peers += [(s, (yy + dy) % 4 * 2 + (zh + dz) % 2) for dy, dz in far_first[:7]]
    for peer in peers:
        pl.semaphore_signal(barrier, inc=1, device_id=peer, device_id_type=MESH)

    pairs = [(x_hbm, x_ref), (y_hbm, y_ref), (diag_hbm, diag), (links_hbm, links), (stiff_hbm, stiff), (att_hbm, owner_row)]
    pairs += [(tiles_hbm.at[pl.ds(i * 11, 11)], tiles.at[pl.ds(i * 11, 11)]) for i in range(4)]
    loads = [pltpu.make_async_copy(a, b, load.at[i]) for i, (a, b) in enumerate(pairs)]
    for i in (5, 0, 6, 7, 8, 9, 1, 2, 3, 4):
        loads[i].start()

    def copy(i, src, dst, seg, vec=None):
        return pltpu.make_async_remote_copy(
            src_ref=src, dst_ref=dst, send_sem=send.at[i], recv_sem=recv.at[i],
            device_id=(seg, v if vec is None else vec), device_id_type=MESH,
        )

    def go(i, src, dst, seg, vec=None):
        c = copy(i, src, dst, seg, vec)
        c.start()
        started.append(c)

    def got(i, dst):
        copy(i, dst, dst, partner).wait_recv()

    lane = lax.broadcasted_iota(I32, (COLS, PANEL), 1)
    c0 = counts[0, 0]

    def block_of(owner):
        return owner % 2 * 32 + owner // 2 % 4 * 8 + owner // 8

    runs = ((z // 2 * 2, 2), (flip(z, 2) // 2 * 2, 2), (flip(z, 4) // 4 * 4, 4))

    def ag_start(r, g, mode):
        g[64] = jnp.zeros((COLS, MB), BF16)
        mine = core * 32 + x * 8 + z
        g[mine] = mode.astype(BF16)
        for k in (7, 6, 5, 4, 3, 2, 1):
            go(AG[r] + k, g.at[mine], g.at[mine], seg_of(z_of[k], x, core))

    def ag_x(r, g, piece):
        for k in ((1,), (2, 3), (4, 5, 6, 7))[piece]:
            got(AG[r] + k, g.at[core * 32 + x * 8 + z_of[k]])
        run = g.at[pl.ds(core * 32 + x * 8 + runs[piece][0], runs[piece][1])]
        for d in (2, 1, 3):
            go(AG[r] + 8 + piece * 3 + d - 1, run, run, seg_of(z, x_of[d], core))

    def ag_core(r, g):
        for d in (0, 1, 3, 2):
            row = core * 32 + x_of[-d % 4] * 8
            for piece in range(3) if d else ():
                got(AG[r] + 8 + piece * 3 + d - 1, g.at[pl.ds(row + runs[piece][0], runs[piece][1])])
            whole = g.at[pl.ds(row, 8)]
            go(AG[r] + 17 + d, whole, whole, partner)

    def ag_end(r, g):
        for d in (0, 1, 3, 2):
            got(AG[r] + 17 + d, g.at[pl.ds(pc * 32 + x_of[-d % 4] * 8, 8)])

    def outgoing(src, low, high):
        def one(t, _):
            slot = jnp.minimum(jnp.where(t < c0, t, t - c0 + PANELS), SLOTS - 1)
            out[t] = jnp.dot(src[slot].astype(BF16), tiles[t], preferred_element_type=F32).astype(BF16)
            return 0

        lax.fori_loop(low, high, one, 0, unroll=4 if high - low == 44 else high - low)

    def sums(r, cc, k):
        def one(xx, _):
            b = cc * 32 + xx * 8 + z_of[k]
            s_buf[r, cc, xx, z_of[k]] = out[tab[0, b, 0]].astype(F32) + out[tab[1, b, 0]].astype(F32)
            return 0

        lax.fori_loop(0, 4, one, 0, unroll=True)

    def rs_core(r, k):
        go(RS[r] + k, s_buf.at[r, pc, :, z_of[k]], c_buf.at[r, :, z_of[k]], partner)

    def add_core(r, k):
        zk = z_of[k]
        got(RS[r] + k, c_buf.at[r, :, zk])
        for xx in range(4):
            s_buf[r, core, xx, zk] = s_buf[r, core, xx, zk] + c_buf[r, xx, zk]

    def rs_x1(r, k):
        add_core(r, k)
        via = 3 if k % 2 else 1
        for n, to, d in ((0, 2, via), (1, 4 - via, 4 - via)):
            src = s_buf.at[r, core, x_of[to], z_of[k]]
            go(RS[r] + 10 + k * 3 + n, src, r_buf.at[r, n, k], seg_of(z, x_of[d], core))

    def rs_x2(r, k):
        to = x_of[3 if k % 2 else 1]
        got(RS[r] + 10 + k * 3, r_buf.at[r, 0, k])
        s_buf[r, core, to, z_of[k]] = s_buf[r, core, to, z_of[k]] + r_buf[r, 0, k]
        go(RS[r] + 12 + k * 3, s_buf.at[r, core, to, z_of[k]], r_buf.at[r, 2, k], seg_of(z, to, core))

    def rs_z(r, k):
        zk = z_of[k]
        total = s_buf[r, core, x, zk]
        for n in (1, 2):
            got(RS[r] + 10 + k * 3 + n, r_buf.at[r, n, k])
            total = total + r_buf[r, n, k]
        s_buf[r, core, x, zk] = total
        if k % 4:
            go(RS[r] + 34 + k, s_buf.at[r, core, x, zk], z_buf.at[r, k], seg_of(z_of[k % 4], x, core))

    def rs_far(r):
        total = s_buf[r, core, x, z_of[4]]
        for k in (5, 6, 7):
            got(RS[r] + 34 + k, z_buf.at[r, k])
            total = total + z_buf[r, k]
        s_buf[r, core, x, z_of[4]] = total
        go(RS[r] + 38, s_buf.at[r, core, x, z_of[4]], z_buf.at[r, 4], seg_of(z_of[4], x, core))

    def rs_end(r):
        total = s_buf[r, core, x, z]
        for k in (1, 2, 3, 4):
            got(RS[r] + 34 + k, z_buf.at[r, k])
            total = total + z_buf[r, k]
        return total

    def halo_send(r, src):
        halo[r, 2] = src[SLOTS - 1] * links[pl.ds(SLOTS - 1, 1), :]
        go(HALO[r], src.at[0], halo.at[r, 0], (s + 63) % 64)
        go(HALO[r] + 1, halo.at[r, 2], halo.at[r, 1], (s + 1) % 64)

    def halo_take(r, src):
        got(HALO[r], halo.at[r, 0])
        got(HALO[r] + 1, halo.at[r, 1])
        src[SLOTS] = jnp.where(s < 63, halo[r, 0], 0.0)
        halo[r, 3] = jnp.where(s > 0, halo[r, 1], 0.0)

    def shifted(r, src, g, q, before):
        here = src[q]
        link = links[pl.ds(q, 1), :]
        linked = link * here
        after = jnp.where(lane == PANEL - 1, pltpu.roll(src[q + 1], PANEL - 1, 1), pltpu.roll(here, PANEL - 1, 1))
        prior = jnp.where(lane == 0, pltpu.roll(before, 1, 1), pltpu.roll(linked, 1, 1))
        second = q >= PANELS
        rank = jnp.where(second, q - PANELS, q)
        t = jnp.minimum(jnp.where(second, rank + c0, rank), ATT - 1)
        used = rank < jnp.where(second, counts[0, 1], c0)
        block = jnp.where(used, block_of(att[0, t]), 64)
        coupled = lax.dot_general(g[block], tiles[t], NT, preferred_element_type=F32)
        return (diag[pl.ds(q, 1), :] - 3.0) * here - link * after - prior + coupled, linked

    def stiffened(mode):
        wide = jnp.concatenate([stiff[pl.ds(0, 1), :], stiff[pl.ds(1, 1), :]], 1) - 3.0
        return wide * mode

    loads[5].wait()
    owner = owner_row[...]
    at = lax.broadcasted_iota(I32, (64, ATT), 1)
    same = jnp.broadcast_to(block_of(owner), (64, ATT)) == lax.broadcasted_iota(I32, (64, ATT), 0)
    one = jnp.min(jnp.where(same, at, ATT), 1, keepdims=True)
    two = jnp.max(jnp.where(same, at, -1), 1, keepdims=True)
    tab_v[0] = jnp.broadcast_to(one, (64, 128))
    tab_v[1] = jnp.broadcast_to(jnp.where(two > one, two, ATT), (64, 128))
    to_scalars = pltpu.make_async_copy(tab_v, tab, load.at[10])
    to_scalars.start()
    out[ATT] = jnp.zeros((COLS, MB), BF16)
    loads[0].wait()
    for q in range(SLOTS):
        xe[q] = x_ref[:, q * PANEL : (q + 1) * PANEL]
    for i in range(4):
        loads[6 + i].wait()
        outgoing(xe, i * 11, i * 11 + 11)
    to_scalars.wait()
    for i in range(1, 5):
        loads[i].wait()
    for k in ORDER:
        sums(0, pc, k)
        sums(0, core, k)
    pl.semaphore_wait(barrier, len(peers))
    for k in ORDER[:2]:
        rs_core(0, k)
    ag_start(0, g1, y_ref[...])
    for k in ORDER[2:]:
        rs_core(0, k)
    for k in (7, 6, 5, 4):
        rs_x1(0, k)
    halo_send(0, xe)
    ag_x(0, g1, 0)
    ag_x(0, g1, 1)
    for k in (7, 6, 5, 4):
        rs_x2(0, k)
    for k in (3, 2, 1, 0):
        rs_x1(0, k)
    ag_x(0, g1, 2)
    for k in (7, 6, 5, 4):
        rs_z(0, k)
    for k in (3, 2, 1, 0):
        rs_x2(0, k)
    ag_core(0, g1)
    rs_far(0)
    for k in (3, 2, 1, 0):
        rs_z(0, k)
    halo_take(0, xe)
    ag_end(0, g1)

    def first_panel(q, before):
        image, linked = shifted(0, xe, g1, q, before)
        we[q] = image * 0.4
        return linked

    lax.fori_loop(0, SLOTS, first_panel, halo[0, 3], unroll=4)
    halo_send(1, we)

    outgoing(we, 0, 44)
    for k in ORDER:
        sums(1, pc, k)
        rs_core(1, k)
    for k in ORDER:
        sums(1, core, k)
    w_mode[...] = (stiffened(y_ref[...]) + rs_end(0)) * 0.4
    ag_start(1, g2, w_mode[...])
    for k in ORDER[:6]:
        rs_x1(1, k)
    for k in (7, 6, 5, 4):
        rs_x2(1, k)
    ag_x(1, g2, 0)
    ag_x(1, g2, 1)
    rs_x1(1, 1)
    rs_x1(1, 0)
    ag_x(1, g2, 2)
    for k in (7, 6, 5, 4):
        rs_z(1, k)
    for k in (3, 2, 1, 0):
        rs_x2(1, k)
    rs_far(1)
    ag_core(1, g2)
    for k in (3, 2, 1, 0):
        rs_z(1, k)
    halo_take(1, we)
    ag_end(1, g2)

    def second_panel(q, before):
        image, linked = shifted(1, we, g2, q, before)
        value = image * 0.8 - xe[q]
        line_out[:, pl.ds(pl.multiple_of(q * PANEL, PANEL), PANEL)] = value
        fb[q] = value.astype(BF16)
        return linked

    def row_chunk(dy, dz):
        k = (yy + dy) % 4 * 2 + (zh + dz) % 2
        q0 = k * 6
        ahead = jnp.maximum(q0 - 1, 0)
        before = jnp.where(q0 > 0, links[pl.ds(ahead, 1), :] * we[ahead], halo[1, 3])
        lax.fori_loop(0, 6, lambda i, b: second_panel(q0 + i, b), before, unroll=3)
        if (dy, dz) != (0, 0):
            go(GRAM + dy * 2 + dz, fb.at[pl.ds(q0, 6)], gb.at[v], s, k)

    keeper = s % 8

    def mode_number(one, other):
        return MODE + (one // 2 - other // 2 + 4) % 4 * 2 + (one + other) % 2

    for dy, dz in far_first[:4]:
        row_chunk(dy, dz)
    filtered = (stiffened(w_mode[...]) + rs_end(1)) * 0.8 - y_ref[...]
    mode_out[...] = filtered
    fm[...] = filtered.astype(BF16)

    @pl.when(v != keeper)
    def _():
        copy(mode_number(keeper, v), fm, mb.at[v], s, keeper).start()

    @pl.when(v == keeper)
    def _():
        mb[v] = fm[...]

    for dy, dz in far_first[4:]:
        row_chunk(dy, dz)
    gb[v] = fb[pl.ds(v * 6, 6)]

    for dy, dz in far_first[4:7] + far_first[:4]:
        frm = (yy + 4 - dy) % 4 * 2 + (zh + dz) % 2
        got(GRAM + dy * 2 + dz, gb.at[frm])
    wide = jnp.concatenate([gb[:, p].reshape(8 * COLS, PANEL) for p in range(6)], 1)
    g_acc[...] = lax.dot_general(wide, wide, NT, preferred_element_type=F32)

    @pl.when(v != keeper)
    def _():
        copy(mode_number(keeper, v), fm, mb.at[v], s, keeper).wait_send()

    @pl.when(v == keeper)
    def _():
        for dy, dz in far_first[:7]:
            frm = (yy + 4 - dy) % 4 * 2 + (zh + dz) % 2
            got(MODE + dy * 2 + dz, mb.at[frm])
        modes = mb[...].reshape(8 * COLS, MB)
        g_acc[...] += lax.dot_general(modes, modes, NT, preferred_element_type=F32)

    for y1 in range(4):
        for x1 in range(4):
            for c1 in range(2):
                for h1 in range(2):
                    row = (y1 * 2 + h1) * 32 + x1 * 8
                    p_buf[(y1 * 4 + x1) * 2 + c1, h1] = g_acc[row : row + 8, c1 * 128 : c1 * 128 + 128]

    def plane_copy(r):
        w1 = (yy + r // 8) % 4, (x + r // 2 % 4) % 4, (core + r % 2) % 2
        src = p_buf.at[(w1[0] * 4 + w1[1]) * 2 + w1[2]]
        return copy(PLANE + r, src, p_recv.at[r], seg_of(z, w1[1], w1[2]), w1[0] * 2 + zh)

    def start_plane(r, _):
        plane_copy(r).start()
        return 0

    lax.fori_loop(1, 32, start_plane, 0)

    def take_plane(r, total):
        got(PLANE + r, p_recv.at[r])
        return total + p_recv[r]

    mine = (yy * 4 + x) * 2 + core
    q_buf[...] = lax.fori_loop(1, 32, take_plane, p_buf[mine])

    def z_copy(r):
        u = (zh * 8 + z + r) % 16
        return copy(ZSUM + r, q_buf.at[u // 8], q_recv.at[r], seg_of(u % 8, x, core), yy * 2 + u // 8)

    def start_z(r, _):
        z_copy(r).start()
        return 0

    lax.fori_loop(1, 16, start_z, 0)

    def take_z(r, total):
        got(ZSUM + r, q_recv.at[r])
        return total + q_recv[r]

    j = x * 2 + core
    last[j] = lax.fori_loop(1, 16, take_z, q_buf[zh]) * (1.0 / TOTAL)

    def last_copy(r):
        j1 = (j + r) % 8
        return copy(LAST + r, last.at[j], last.at[j], seg_of(z, j1 // 2, j1 % 2))

    for r in range(1, 8):
        last_copy(r).start()
    for r in range(1, 8):
        got(LAST + r, last.at[(j + 8 - r) % 8])
    for j1 in range(8):
        gram_out[j1 // 2 * 8 : j1 // 2 * 8 + 8, j1 % 2 * 128 : j1 % 2 * 128 + 128] = last[j1]

    for c in started:
        c.wait_send()

    def end_plane(r, _):
        plane_copy(r).wait_send()
        return 0

    lax.fori_loop(1, 32, end_plane, 0)

    def end_z(r, _):
        z_copy(r).wait_send()
        return 0

    lax.fori_loop(1, 16, end_z, 0)
    for r in range(1, 8):
        last_copy(r).wait_send()


def body(line_vectors, mode_vectors, line_diagonal, line_links, stiffness, coupling_tiles, attachments, block_counts):
    block = (COLS, MB)
    owners = attachments.reshape(1, ATT)
    return pl.pallas_call(
        kernel,
        out_shape=(
            jax.ShapeDtypeStruct((COLS, SLOTS * PANEL), F32),
            jax.ShapeDtypeStruct(block, F32),
            jax.ShapeDtypeStruct((COLS, 8 * COLS), F32),
        ),
        in_specs=[pl.BlockSpec(memory_space=pltpu.SMEM)] * 2 + [pl.BlockSpec(memory_space=pltpu.HBM)] * 7,
        out_specs=[pl.BlockSpec(memory_space=pltpu.VMEM)] * 3,
        scratch_shapes=[
            pltpu.VMEM((COLS, SLOTS * PANEL), F32),
            pltpu.VMEM(block, F32),
            pltpu.VMEM((SLOTS, PANEL), F32),
            pltpu.VMEM((SLOTS, PANEL), F32),
            pltpu.VMEM((2, PANEL), F32),
            pltpu.VMEM((ATT, PANEL, MB), BF16),
            pltpu.VMEM((1, ATT), I32),
            pltpu.VMEM((2, 64, 128), I32),
            pltpu.SMEM((2, 64, 128), I32),
            pltpu.VMEM((65,) + block, BF16),
            pltpu.VMEM((65,) + block, BF16),
            pltpu.VMEM((ATT + 1,) + block, BF16),
            pltpu.VMEM((2, 2, 4, 8) + block, F32),
            pltpu.VMEM((2, 4, 8) + block, F32),
            pltpu.VMEM((2, 3, 8) + block, F32),
            pltpu.VMEM((2, 8) + block, F32),
            pltpu.VMEM((SLOTS + 1, COLS, PANEL), F32),
            pltpu.VMEM((SLOTS + 1, COLS, PANEL), F32),
            pltpu.VMEM((2, 4, COLS, PANEL), F32),
            pltpu.VMEM(block, F32),
            pltpu.VMEM((SLOTS, COLS, PANEL), BF16),
            pltpu.VMEM((8, 6, COLS, PANEL), BF16),
            pltpu.VMEM(block, BF16),
            pltpu.VMEM((8,) + block, BF16),
            pltpu.VMEM((256, 256), F32),
            pltpu.VMEM((32, 2, 8, 128), F32),
            pltpu.VMEM((32, 2, 8, 128), F32),
            pltpu.VMEM((2, 8, 128), F32),
            pltpu.VMEM((16, 8, 128), F32),
            pltpu.VMEM((8, 8, 128), F32),
            pltpu.SemaphoreType.DMA((MESSAGES,)),
            pltpu.SemaphoreType.DMA((MESSAGES,)),
            pltpu.SemaphoreType.DMA((11,)),
        ],
        compiler_params=pltpu.CompilerParams(
            has_side_effects=True, collective_id=0, vmem_limit_bytes=64 * 2**20
        ),
    )(
        owners,
        block_counts,
        line_vectors,
        mode_vectors,
        line_diagonal.reshape(SLOTS, PANEL),
        line_links.reshape(SLOTS, PANEL),
        stiffness.reshape(2, PANEL),
        coupling_tiles,
        owners,
    )


def solution(mesh):
    in_specs = (
        P("vec", "seg"),
        P("vec", "seg"),
        P("seg"),
        P("seg"),
        P("seg"),
        P("seg", None, None),
        P("seg", None),
        P("seg", None),
    )
    out_specs = (P("vec", "seg"), P("vec", "seg"), P("vec", None))
    return jax.shard_map(body, mesh=mesh, in_specs=in_specs, out_specs=out_specs, check_vma=False)
```

```python
import jax
import jax.numpy as jnp
from jax import lax
from jax.experimental import pallas as pl
from jax.experimental.pallas import tpu as pltpu
from jax.sharding import PartitionSpec as P

F32 = jnp.float32
BF16 = jnp.bfloat16
I32 = jnp.int32
PANEL = 128
PANELS = 24
SLOTS = 48
ATT = 44
COLS = 32
MB = 256
TOTAL = 393216 + 16384
MESH = pl.DeviceIdType.MESH
NT = (((1,), (1,)), ((), ()))

AG = (0, 24)
RS = (48, 96)
HALO = (144, 146)
GRAM = 152
MODE = 160
PLANE = 168
ZSUM = 200
LAST = 216
MESSAGES = 224
ORDER = (7, 6, 5, 4, 3, 2, 1, 0)


def kernel(
    att, counts, x_hbm, y_hbm, diag_hbm, links_hbm, stiff_hbm, tiles_hbm, att_hbm,
    line_out, mode_out, gram_out,
    x_ref, y_ref, diag, links, stiff, tiles, owner_row, tab_v, tab,
    g1, g2, out, s_buf, c_buf, r_buf, z_buf, xe, we, halo, w_mode, fb, gb, fm, mb, g_acc, p_buf, p_core, p_recv, q_buf, q_recv, last,
    send, recv, load,
):
    s = lax.axis_index("seg")
    v = lax.axis_index("vec")
    core, x, z = s % 2, s // 2 % 4, s // 8
    yy, zh = v // 2, v % 2
    pc = 1 - core
    started = []

    def seg_of(zz, xx, cc):
        return zz * 8 + xx * 2 + cc

    def flip(a, n):
        for bit in (1, 2, 4):
            if n & bit:
                a = a + bit - 2 * bit * (a // bit % 2)
        return a

    partner = seg_of(z, x, pc)
    x_of = [(x + d) % 4 for d in range(4)]
    z_of = [flip(z, k) for k in range(8)]
    far_first = ((0, 1), (1, 1), (2, 1), (3, 1), (1, 0), (2, 0), (3, 0), (0, 0))

    barrier = pltpu.get_barrier_semaphore()
    peers = [(partner, v), ((s + 1) % 64, v), ((s + 63) % 64, v)]
    peers += [(seg_of(z, x_of[d], core), v) for d in (1, 2, 3)]
    peers += [(seg_of(z_of[k], x, core), v) for k in range(1, 8)]
    peers += [(s, (yy + dy) % 4 * 2 + (zh + dz) % 2) for dy, dz in far_first[:7]]
    for peer in peers:
        pl.semaphore_signal(barrier, inc=1, device_id=peer, device_id_type=MESH)

    pairs = [(x_hbm, x_ref), (y_hbm, y_ref), (diag_hbm, diag), (links_hbm, links), (stiff_hbm, stiff), (att_hbm, owner_row)]
    pairs += [(tiles_hbm.at[pl.ds(i * 11, 11)], tiles.at[pl.ds(i * 11, 11)]) for i in range(4)]
    loads = [pltpu.make_async_copy(a, b, load.at[i]) for i, (a, b) in enumerate(pairs)]
    for i in (5, 0, 6, 7, 8, 9, 1, 2, 3, 4):
        loads[i].start()

    def copy(i, src, dst, seg, vec=None):
        return pltpu.make_async_remote_copy(
            src_ref=src, dst_ref=dst, send_sem=send.at[i], recv_sem=recv.at[i],
            device_id=(seg, v if vec is None else vec), device_id_type=MESH,
        )

    def go(i, src, dst, seg, vec=None):
        c = copy(i, src, dst, seg, vec)
        c.start()
        started.append(c)

    def got(i, dst):
        copy(i, dst, dst, partner).wait_recv()

    lane = lax.broadcasted_iota(I32, (COLS, PANEL), 1)
    c0 = counts[0, 0]

    def block_of(owner):
        return owner % 2 * 32 + owner // 2 % 4 * 8 + owner // 8

    runs = [flip(z, k) // 2 * 2 for k in (0, 2, 4, 6)]

    def ag_start(r, g, mode):
        g[64] = jnp.zeros((COLS, MB), BF16)
        mine = core * 32 + x * 8 + z
        g[mine] = mode.astype(BF16)
        for k in (7, 6, 5, 4, 3, 2, 1):
            go(AG[r] + k, g.at[mine], g.at[mine], seg_of(z_of[k], x, core))

    def ag_x(r, g, piece):
        for k in ((1,), (2, 3), (4, 5), (6, 7))[piece]:
            got(AG[r] + k, g.at[core * 32 + x * 8 + z_of[k]])
        run = g.at[pl.ds(core * 32 + x * 8 + runs[piece], 2)]
        for d in (2, 1, 3):
            go(AG[r] + 8 + piece * 3 + d - 1, run, run, seg_of(z, x_of[d], core))

    def ag_core(r, g):
        for d in (0, 1, 3, 2):
            row = core * 32 + x_of[-d % 4] * 8
            for piece in range(4) if d else ():
                got(AG[r] + 8 + piece * 3 + d - 1, g.at[pl.ds(row + runs[piece], 2)])
            whole = g.at[pl.ds(row, 8)]
            go(AG[r] + 20 + d, whole, whole, partner)

    def ag_end(r, g):
        for d in (0, 1, 3, 2):
            got(AG[r] + 20 + d, g.at[pl.ds(pc * 32 + x_of[-d % 4] * 8, 8)])

    def outgoing(src, low, high):
        def one(t, _):
            slot = jnp.minimum(jnp.where(t < c0, t, t - c0 + PANELS), SLOTS - 1)
            out[t] = jnp.dot(src[slot].astype(BF16), tiles[t], preferred_element_type=F32).astype(BF16)
            return 0

        lax.fori_loop(low, high, one, 0, unroll=11)

    def sums(r, cc, k):
        def one(xx, _):
            b = cc * 32 + xx * 8 + z_of[k]
            s_buf[r, cc, xx, z_of[k]] = out[tab[0, b, 0]].astype(F32) + out[tab[1, b, 0]].astype(F32)
            return 0

        lax.fori_loop(0, 4, one, 0, unroll=True)

    def rs_core(r, k):
        go(RS[r] + k, s_buf.at[r, pc, :, z_of[k]], c_buf.at[r, :, z_of[k]], partner)

    def add_core(r, k):
        zk = z_of[k]
        got(RS[r] + k, c_buf.at[r, :, zk])
        for xx in range(4):
            s_buf[r, core, xx, zk] = s_buf[r, core, xx, zk] + c_buf[r, xx, zk]

    def rs_x1(r, k):
        add_core(r, k)
        via = 3 if k % 2 else 1
        for n, to, d in ((0, 2, via), (1, 4 - via, 4 - via)):
            src = s_buf.at[r, core, x_of[to], z_of[k]]
            go(RS[r] + 10 + k * 3 + n, src, r_buf.at[r, n, k], seg_of(z, x_of[d], core))

    def rs_x2(r, k):
        to = x_of[3 if k % 2 else 1]
        got(RS[r] + 10 + k * 3, r_buf.at[r, 0, k])
        s_buf[r, core, to, z_of[k]] = s_buf[r, core, to, z_of[k]] + r_buf[r, 0, k]
        go(RS[r] + 12 + k * 3, s_buf.at[r, core, to, z_of[k]], r_buf.at[r, 2, k], seg_of(z, to, core))

    def rs_z(r, k):
        zk = z_of[k]
        total = s_buf[r, core, x, zk]
        for n in (1, 2):
            got(RS[r] + 10 + k * 3 + n, r_buf.at[r, n, k])
            total = total + r_buf[r, n, k]
        s_buf[r, core, x, zk] = total
        if k % 4:
            go(RS[r] + 34 + k, s_buf.at[r, core, x, zk], z_buf.at[r, k], seg_of(z_of[k % 4], x, core))

    def rs_far(r):
        total = s_buf[r, core, x, z_of[4]]
        for k in (5, 6, 7):
            got(RS[r] + 34 + k, z_buf.at[r, k])
            total = total + z_buf[r, k]
        s_buf[r, core, x, z_of[4]] = total
        go(RS[r] + 38, s_buf.at[r, core, x, z_of[4]], z_buf.at[r, 4], seg_of(z_of[4], x, core))

    def rs_end(r):
        total = s_buf[r, core, x, z]
        for k in (1, 2, 3, 4):
            got(RS[r] + 34 + k, z_buf.at[r, k])
            total = total + z_buf[r, k]
        return total

    def halo_send(r, src):
        halo[r, 2] = src[SLOTS - 1] * links[pl.ds(SLOTS - 1, 1), :]
        go(HALO[r], src.at[0], halo.at[r, 0], (s + 63) % 64)
        go(HALO[r] + 1, halo.at[r, 2], halo.at[r, 1], (s + 1) % 64)

    def halo_take(r, src):
        got(HALO[r], halo.at[r, 0])
        got(HALO[r] + 1, halo.at[r, 1])
        src[SLOTS] = jnp.where(s < 63, halo[r, 0], 0.0)
        halo[r, 3] = jnp.where(s > 0, halo[r, 1], 0.0)

    def shifted(r, src, g, q, before):
        here = src[q]
        link = links[pl.ds(q, 1), :]
        linked = link * here
        after = jnp.where(lane == PANEL - 1, pltpu.roll(src[q + 1], PANEL - 1, 1), pltpu.roll(here, PANEL - 1, 1))
        prior = jnp.where(lane == 0, pltpu.roll(before, 1, 1), pltpu.roll(linked, 1, 1))
        second = q >= PANELS
        rank = jnp.where(second, q - PANELS, q)
        t = jnp.minimum(jnp.where(second, rank + c0, rank), ATT - 1)
        used = rank < jnp.where(second, counts[0, 1], c0)
        block = jnp.where(used, block_of(att[0, t]), 64)
        coupled = lax.dot_general(g[block], tiles[t], NT, preferred_element_type=F32)
        return (diag[pl.ds(q, 1), :] - 3.0) * here - link * after - prior + coupled, linked

    def stiffened(mode):
        wide = jnp.concatenate([stiff[pl.ds(0, 1), :], stiff[pl.ds(1, 1), :]], 1) - 3.0
        return wide * mode

    loads[5].wait()
    owner = owner_row[...]
    at = lax.broadcasted_iota(I32, (64, ATT), 1)
    same = jnp.broadcast_to(block_of(owner), (64, ATT)) == lax.broadcasted_iota(I32, (64, ATT), 0)
    one = jnp.min(jnp.where(same, at, ATT), 1, keepdims=True)
    two = jnp.max(jnp.where(same, at, -1), 1, keepdims=True)
    tab_v[0] = jnp.broadcast_to(one, (64, 128))
    tab_v[1] = jnp.broadcast_to(jnp.where(two > one, two, ATT), (64, 128))
    to_scalars = pltpu.make_async_copy(tab_v, tab, load.at[10])
    to_scalars.start()
    out[ATT] = jnp.zeros((COLS, MB), BF16)
    loads[0].wait()
    for q in range(SLOTS):
        xe[q] = x_ref[:, q * PANEL : (q + 1) * PANEL]
    for i in range(4):
        loads[6 + i].wait()
        outgoing(xe, i * 11, i * 11 + 11)
    to_scalars.wait()
    for i in range(1, 5):
        loads[i].wait()
    for k in ORDER:
        sums(0, pc, k)
        sums(0, core, k)
    pl.semaphore_wait(barrier, len(peers))
    for k in ORDER[:2]:
        rs_core(0, k)
    ag_start(0, g1, y_ref[...])
    for k in ORDER[2:]:
        rs_core(0, k)
    for k in (7, 6, 5, 4):
        rs_x1(0, k)
    halo_send(0, xe)
    ag_x(0, g1, 0)
    ag_x(0, g1, 1)
    for k in (7, 6, 5, 4):
        rs_x2(0, k)
    for k in (3, 2, 1, 0):
        rs_x1(0, k)
    ag_x(0, g1, 2)
    ag_x(0, g1, 3)
    for k in (7, 6, 5, 4):
        rs_z(0, k)
    for k in (3, 2, 1, 0):
        rs_x2(0, k)
    ag_core(0, g1)
    rs_far(0)
    for k in (3, 2, 1, 0):
        rs_z(0, k)
    halo_take(0, xe)
    ag_end(0, g1)

    def first_panel(q, before):
        image, linked = shifted(0, xe, g1, q, before)
        we[q] = image * 0.4
        return linked

    lax.fori_loop(0, SLOTS, first_panel, halo[0, 3], unroll=12)
    halo_send(1, we)

    outgoing(we, 0, 44)
    for k in ORDER:
        sums(1, pc, k)
        rs_core(1, k)
    for k in ORDER:
        sums(1, core, k)
    w_mode[...] = (stiffened(y_ref[...]) + rs_end(0)) * 0.4
    ag_start(1, g2, w_mode[...])
    for k in ORDER[:6]:
        rs_x1(1, k)
    for k in (7, 6, 5, 4):
        rs_x2(1, k)
    ag_x(1, g2, 0)
    ag_x(1, g2, 1)
    rs_x1(1, 1)
    rs_x1(1, 0)
    ag_x(1, g2, 2)
    ag_x(1, g2, 3)
    for k in (7, 6, 5, 4):
        rs_z(1, k)
    for k in (3, 2, 1, 0):
        rs_x2(1, k)
    rs_far(1)
    ag_core(1, g2)
    for k in (3, 2, 1, 0):
        rs_z(1, k)
    halo_take(1, we)
    ag_end(1, g2)

    def second_panel(q, before):
        image, linked = shifted(1, we, g2, q, before)
        value = image * 0.8 - xe[q]
        line_out[:, pl.ds(pl.multiple_of(q * PANEL, PANEL), PANEL)] = value
        fb[q] = value.astype(BF16)
        return linked

    def row_chunk(dy, dz):
        k = (yy + dy) % 4 * 2 + (zh + dz) % 2
        q0 = k * 6
        ahead = jnp.maximum(q0 - 1, 0)
        before = jnp.where(q0 > 0, links[pl.ds(ahead, 1), :] * we[ahead], halo[1, 3])
        lax.fori_loop(0, 6, lambda i, b: second_panel(q0 + i, b), before, unroll=True)
        if (dy, dz) != (0, 0):
            go(GRAM + dy * 2 + dz, fb.at[pl.ds(q0, 6)], gb.at[v], s, k)

    keeper = s % 8

    def mode_number(one, other):
        return MODE + (one // 2 - other // 2 + 4) % 4 * 2 + (one + other) % 2

    for dy, dz in far_first[:4]:
        row_chunk(dy, dz)
    filtered = (stiffened(w_mode[...]) + rs_end(1)) * 0.8 - y_ref[...]
    mode_out[...] = filtered
    fm[...] = filtered.astype(BF16)

    @pl.when(v != keeper)
    def _():
        copy(mode_number(keeper, v), fm, mb.at[v], s, keeper).start()

    @pl.when(v == keeper)
    def _():
        mb[v] = fm[...]

    for dy, dz in far_first[4:]:
        row_chunk(dy, dz)
    gb[v] = fb[pl.ds(v * 6, 6)]

    for dy, dz in far_first[4:7] + far_first[:4]:
        frm = (yy + 4 - dy) % 4 * 2 + (zh + dz) % 2
        got(GRAM + dy * 2 + dz, gb.at[frm])
    wide = jnp.concatenate([gb[:, p].reshape(8 * COLS, PANEL) for p in range(6)], 1)
    g_acc[...] = lax.dot_general(wide, wide, NT, preferred_element_type=F32)

    @pl.when(v != keeper)
    def _():
        copy(mode_number(keeper, v), fm, mb.at[v], s, keeper).wait_send()

    @pl.when(v == keeper)
    def _():
        for dy, dz in far_first[:7]:
            frm = (yy + 4 - dy) % 4 * 2 + (zh + dz) % 2
            got(MODE + dy * 2 + dz, mb.at[frm])
        modes = mb[...].reshape(8 * COLS, MB)
        g_acc[...] += lax.dot_general(modes, modes, NT, preferred_element_type=F32)

    for y1 in range(4):
        for x1 in range(4):
            for c1 in range(2):
                for h1 in range(2):
                    row = (y1 * 2 + h1) * 32 + x1 * 8
                    p_buf[c1 * 16 + y1 * 4 + x1, h1] = g_acc[row : row + 8, c1 * 128 : c1 * 128 + 128]

    go(PLANE, p_buf.at[pl.ds(pc * 16, 16)], p_core, partner)
    got(PLANE, p_core)
    for i in range(16):
        p_buf[core * 16 + i] = p_buf[core * 16 + i] + p_core[i]

    def plane_copy(r):
        y1, x1 = (yy + r // 4) % 4, (x + r % 4) % 4
        src = p_buf.at[core * 16 + y1 * 4 + x1]
        return copy(PLANE + r, src, p_recv.at[r], seg_of(z, x1, core), y1 * 2 + zh)

    for r in (10, 9, 11, 6, 14, 5, 7, 13, 15, 2, 8, 1, 3, 4, 12):
        plane_copy(r).start()
    total = p_buf[core * 16 + yy * 4 + x]
    for r in range(1, 16):
        got(PLANE + r, p_recv.at[r])
        total = total + p_recv[r]
    q_buf[...] = total

    def z_copy(r):
        u = (zh * 8 + z + r) % 16
        return copy(ZSUM + r, q_buf.at[u // 8], q_recv.at[r], seg_of(u % 8, x, core), yy * 2 + u // 8)

    def start_z(r, _):
        z_copy(r).start()
        return 0

    lax.fori_loop(1, 16, start_z, 0, unroll=True)

    def take_z(r, total):
        got(ZSUM + r, q_recv.at[r])
        return total + q_recv[r]

    j = x * 2 + core
    last[j] = lax.fori_loop(1, 16, take_z, q_buf[zh], unroll=True) * (1.0 / TOTAL)

    def last_copy(r):
        j1 = (j + r) % 8
        return copy(LAST + r, last.at[j], last.at[j], seg_of(z, j1 // 2, j1 % 2))

    for r in range(1, 8):
        last_copy(r).start()
    for r in range(1, 8):
        got(LAST + r, last.at[(j + 8 - r) % 8])
    for j1 in range(8):
        gram_out[j1 // 2 * 8 : j1 // 2 * 8 + 8, j1 % 2 * 128 : j1 % 2 * 128 + 128] = last[j1]

    for c in started:
        c.wait_send()

    for r in range(1, 16):
        plane_copy(r).wait_send()

    def end_z(r, _):
        z_copy(r).wait_send()
        return 0

    lax.fori_loop(1, 16, end_z, 0, unroll=True)
    for r in range(1, 8):
        last_copy(r).wait_send()


def body(line_vectors, mode_vectors, line_diagonal, line_links, stiffness, coupling_tiles, attachments, block_counts):
    block = (COLS, MB)
    owners = attachments.reshape(1, ATT)
    return pl.pallas_call(
        kernel,
        out_shape=(
            jax.ShapeDtypeStruct((COLS, SLOTS * PANEL), F32),
            jax.ShapeDtypeStruct(block, F32),
            jax.ShapeDtypeStruct((COLS, 8 * COLS), F32),
        ),
        in_specs=[pl.BlockSpec(memory_space=pltpu.SMEM)] * 2 + [pl.BlockSpec(memory_space=pltpu.HBM)] * 7,
        out_specs=[pl.BlockSpec(memory_space=pltpu.VMEM)] * 3,
        scratch_shapes=[
            pltpu.VMEM((COLS, SLOTS * PANEL), F32),
            pltpu.VMEM(block, F32),
            pltpu.VMEM((SLOTS, PANEL), F32),
            pltpu.VMEM((SLOTS, PANEL), F32),
            pltpu.VMEM((2, PANEL), F32),
            pltpu.VMEM((ATT, PANEL, MB), BF16),
            pltpu.VMEM((1, ATT), I32),
            pltpu.VMEM((2, 64, 128), I32),
            pltpu.SMEM((2, 64, 128), I32),
            pltpu.VMEM((65,) + block, BF16),
            pltpu.VMEM((65,) + block, BF16),
            pltpu.VMEM((ATT + 1,) + block, BF16),
            pltpu.VMEM((2, 2, 4, 8) + block, F32),
            pltpu.VMEM((2, 4, 8) + block, F32),
            pltpu.VMEM((2, 3, 8) + block, F32),
            pltpu.VMEM((2, 8) + block, F32),
            pltpu.VMEM((SLOTS + 1, COLS, PANEL), F32),
            pltpu.VMEM((SLOTS + 1, COLS, PANEL), F32),
            pltpu.VMEM((2, 4, COLS, PANEL), F32),
            pltpu.VMEM(block, F32),
            pltpu.VMEM((SLOTS, COLS, PANEL), BF16),
            pltpu.VMEM((8, 6, COLS, PANEL), BF16),
            pltpu.VMEM(block, BF16),
            pltpu.VMEM((8,) + block, BF16),
            pltpu.VMEM((256, 256), F32),
            pltpu.VMEM((32, 2, 8, 128), F32),
            pltpu.VMEM((16, 2, 8, 128), F32),
            pltpu.VMEM((16, 2, 8, 128), F32),
            pltpu.VMEM((2, 8, 128), F32),
            pltpu.VMEM((16, 8, 128), F32),
            pltpu.VMEM((8, 8, 128), F32),
            pltpu.SemaphoreType.DMA((MESSAGES,)),
            pltpu.SemaphoreType.DMA((MESSAGES,)),
            pltpu.SemaphoreType.DMA((11,)),
        ],
        compiler_params=pltpu.CompilerParams(
            has_side_effects=True, collective_id=0, vmem_limit_bytes=64 * 2**20
        ),
    )(
        owners,
        block_counts,
        line_vectors,
        mode_vectors,
        line_diagonal.reshape(SLOTS, PANEL),
        line_links.reshape(SLOTS, PANEL),
        stiffness.reshape(2, PANEL),
        coupling_tiles,
        owners,
    )


def solution(mesh):
    in_specs = (
        P("vec", "seg"),
        P("vec", "seg"),
        P("seg"),
        P("seg"),
        P("seg"),
        P("seg", None, None),
        P("seg", None),
        P("seg", None),
    )
    out_specs = (P("vec", "seg"), P("vec", "seg"), P("vec", None))
    return jax.shard_map(body, mesh=mesh, in_specs=in_specs, out_specs=out_specs, check_vma=False)
```
